32 devices in a mesh: wide: 16 (over z, x, core), narrow: 2 (over y).
Axes of the slice: x: 2, y: 2, z: 4, core: 2. Of those that a mesh axis runs over, the one named last changes fastest.
Arguments:
- wavefunction: float32 [2097152], P(('wide', 'narrow')), may hold values from -6 to 6
- propagator: float32 [705432], replicated, may hold values from -2.5 to 3.5, as said below
- gate_orders: int32 [6, 11], replicated, may hold values from 0 to 10, each once within a row
- sector_order: int32 [2048], replicated, may hold values from 0 to 2047, as said below
- bond_level: int32 [20], replicated, may hold values from -3 to 3
Outputs:
- evolved: float32 [2097152], P(('wide', 'narrow'))
The draws below stay inside these ranges and needn't reach their ends.
Inputs may be any that keep to these rules, and one draw needn't show every extreme that they name: `propagator`: sector blocks for k = 0 .. 11 set bits, each row-major, one after another in increasing k. `sector_order`: a permutation of 0 .. 2047 listing states with fewer set bits first.
All inputs are finite; a program needn't handle non-finite values.
Results may differ from the reference program's by a relative error of at most 0.0001.
Values sent between devices are 32-bit elements; how exact they have to be, the bound alone decides.
A program may use at most 64 MiB of HBM per device.

```python
import math
import jax
import jax.numpy as jnp
from jax import lax

LB = 16
GS = 11
GATES = 6
SITES = 21
AMPS = 2097152
STATES = 2048
N_WIDE = 16
N_NARROW = 2


def draw_propagator(key, part):
    blocks_list = []
    for degree in range(GS + 1):
        sector_size = math.comb(GS, degree)
        sub_key = jax.random.fold_in(key, degree + 17)
        entries = jnp.clip(jax.random.normal(sub_key, (sector_size, sector_size), jnp.float32), -4.0, 4.0)
        symmetric = 0.3 * (entries + entries.T) / math.sqrt(sector_size)
        blocks_list.append((jnp.eye(sector_size, dtype=jnp.float32) + symmetric).reshape(-1))
    return jnp.concatenate(blocks_list)


def draw_sector_order(key, part):
    states = jnp.arange(STATES, dtype=jnp.int32)
    weight = jnp.zeros_like(states)
    for position in range(GS):
        weight = weight + (jnp.right_shift(states, position) & 1)
    shuffle = jax.random.permutation(jax.random.fold_in(key, 5), STATES).astype(jnp.int32)
    scores = weight * STATES + shuffle
    return jnp.argsort(scores, stable=True).astype(jnp.int32)


def with_ends(array, stream_key, smallest, high):
    spot = [jax.random.randint(jax.random.fold_in(stream_key, axis), (), 0, length) for axis, length in enumerate(array.shape)]
    widest = array.shape.index(max(array.shape))
    neighbour = spot[:widest] + [(spot[widest] + 1) % array.shape[widest]] + spot[widest + 1:]
    return array.at[tuple(spot)].set(smallest).at[tuple(neighbour)].set(high)


def block_scale(rng, dims, shards, smallest, largest):
    gain, own = 1.0, jax.random.fold_in(rng, 6)
    for dim, shards_of in shards:
        steps = jnp.exp(jax.random.uniform(jax.random.fold_in(own, dim), (shards_of,), jnp.float32, smallest / len(shards), largest / len(shards)))
        gain = gain * jnp.repeat(steps, dims[dim] // shards_of).reshape([-1 if axis == dim else 1 for axis in range(len(dims))])
    return gain


def centred(key, extent, deviation, bound, shards=(), held_as=jnp.bfloat16):
    result = deviation * jax.random.normal(key, extent, jnp.float32)
    if shards:
        result = result * block_scale(key, extent, shards, -0.22, 0.18)
    return jnp.clip(result, -bound, bound).astype(held_as)


def setup_inputs(seed: int = 0) -> dict:
    key_list = jax.random.split(jax.random.key(seed), 6)
    return {
        "wavefunction": centred(key_list[0], (AMPS,), 1.0, 6.0, ((0, 32),), jnp.float32),
        "propagator": draw_propagator(jax.random.fold_in(key_list[5], 71), 0),
        "gate_orders": jax.vmap(lambda own: jax.random.permutation(own, GS))(jax.random.split(key_list[2], GATES)).reshape((GATES, GS)).astype(jnp.int32),
        "sector_order": draw_sector_order(jax.random.fold_in(key_list[5], 71), 0),
        "bond_level": with_ends(jax.random.randint(key_list[4], (SITES - 1,), -3, 4), jax.random.fold_in(key_list[4], 1), -3, 3).astype(jnp.int32),
    }


ZZ_RATE = 0.06
HIGHEST = lax.Precision.HIGHEST


def spin_sign(index_vals, position):
    return 1 - 2 * (jnp.right_shift(index_vals, position) & 1)


def chain_energy(index_vals, levels):
    energy = jnp.zeros(index_vals.shape, jnp.float32)
    for position in range(levels.shape[0]):
        coupled = levels[position] * spin_sign(index_vals, position) * spin_sign(index_vals, position + 1)
        energy = energy + coupled.astype(jnp.float32)
    return energy


def basis_map(gate_row, sector_order):
    mapped = jnp.zeros_like(sector_order)
    for position in range(GS):
        chosen = jnp.right_shift(sector_order, position) & 1
        mapped = mapped + jnp.left_shift(chosen, gate_row[position])
    mapped = mapped.astype(jnp.int32)
    inverse = jnp.argsort(mapped).astype(jnp.int32)
    return mapped, inverse


def sector_blocks(propagator):
    matrices = []
    prop_start = 0
    for degree in range(GS + 1):
        sector_size = math.comb(GS, degree)
        matrices.append(propagator[prop_start:prop_start + sector_size * sector_size].reshape(sector_size, sector_size))
        prop_start += sector_size * sector_size
    return matrices


def apply_middle(amplitudes, maps, matrices):
    mapped, inverse = maps
    packed = jnp.take(amplitudes, mapped, axis=1)
    pieces = []
    row_start = 0
    for matrix in matrices:
        sector_size = matrix.shape[0]
        segment = packed[:, row_start:row_start + sector_size, :]
        pieces.append(jnp.einsum("ij,bjr->bir", matrix, segment, precision=HIGHEST))
        row_start += sector_size
    return jnp.take(jnp.concatenate(pieces, axis=1), inverse, axis=1)


def apply_last(amplitudes, maps, matrices):
    mapped, inverse = maps
    packed = jnp.take(amplitudes, mapped, axis=1)
    pieces = []
    row_start = 0
    for matrix in matrices:
        sector_size = matrix.shape[0]
        segment = packed[:, row_start:row_start + sector_size]
        pieces.append(jnp.einsum("ij,bj->bi", matrix, segment, precision=HIGHEST))
        row_start += sector_size
    return jnp.take(jnp.concatenate(pieces, axis=1), inverse, axis=1)


def reference(wavefunction, propagator, gate_orders, sector_order, bond_level):
    local_size = 2 ** LB
    high_size = AMPS // local_size
    window = 2 ** GS
    lower_size = local_size // window
    left_size = window // (N_NARROW * N_WIDE)
    matrices = sector_blocks(propagator)
    maps = [basis_map(gate_orders[gate_number], sector_order) for gate_number in range(GATES)]
    low_index = jnp.arange(local_size, dtype=jnp.int32)
    high_index = jnp.arange(high_size, dtype=jnp.int32)
    boundary = bond_level[LB - 1] * spin_sign(low_index, LB - 1)
    energy = chain_energy(high_index, bond_level[LB:])[:, None] + chain_energy(low_index, bond_level[:LB - 1])[None, :]
    energy = energy + (spin_sign(high_index, 0)[:, None] * boundary[None, :]).astype(jnp.float32)
    amplitudes = wavefunction.reshape(high_size, local_size) * jnp.exp(-ZZ_RATE * energy)

    def top_gate(values, gate_maps):
        return apply_middle(values.reshape(high_size, window, lower_size), gate_maps, matrices).reshape(high_size, local_size)

    def low_gate(values, gate_maps):
        return apply_last(values.reshape(-1, window), gate_maps, matrices).reshape(high_size, local_size)

    amplitudes = top_gate(amplitudes, maps[0])
    amplitudes = low_gate(amplitudes, maps[1])
    shaped = amplitudes.reshape(N_WIDE, N_NARROW, N_NARROW, N_WIDE, left_size, lower_size)
    moved = jnp.transpose(shaped, (2, 3, 1, 0, 4, 5)).reshape(N_NARROW * N_WIDE, window, lower_size)
    mixed = apply_middle(moved, maps[2], matrices)
    restored = jnp.transpose(mixed.reshape(N_NARROW, N_WIDE, N_NARROW, N_WIDE, left_size, lower_size), (3, 2, 0, 1, 4, 5))
    amplitudes = restored.reshape(high_size, local_size)
    amplitudes = low_gate(amplitudes, maps[3])
    amplitudes = top_gate(amplitudes, maps[4])
    amplitudes = low_gate(amplitudes, maps[5])
    return amplitudes.reshape(-1)
```

```python
import functools
import math

import jax
import jax.numpy as jnp
import numpy as np
from jax import lax
from jax.experimental import pallas as pl
from jax.experimental.pallas import tpu as pltpu
from jax.sharding import PartitionSpec as P

LB = 16
GS = 11
GATES = 6
ZZ_RATE = 0.06
LANES = 128
ROWS = 512
BF = jnp.bfloat16
F32 = jnp.float32


def up(value, unit):
    return -(-value // unit) * unit


RUN_SIZE = [math.comb(9, s) for s in range(10)]
RUN_PAD = [up(n, 16) for n in RUN_SIZE]
RUN_OFF = [sum(RUN_PAD[:s]) for s in range(10)]
SORTED = sum(RUN_PAD)
SORTED_K = up(SORTED, LANES)
GROUPS = [[0, 1, 2], [3], [4], [5], [6], [7], [8], [9, 10, 11]]
GROUP_SIZE = [256, 256, 384, 512, 512, 384, 256, 256]
GROUP_OFF = [sum(GROUP_SIZE[:i]) for i in range(8)]
TOTAL = sum(GROUP_SIZE)
SECTOR = [math.comb(GS, k) for k in range(GS + 1)]
PROP_OFF = [sum(n * n for n in SECTOR[:k]) for k in range(GS + 1)]
SOURCE_ROWS = 5640
WEIGHT = [0, 1, 1, 2]


def layout():
    pieces = []
    sector_row = {}
    for group, sectors in enumerate(GROUPS):
        at = GROUP_OFF[group]
        rows = GROUP_OFF[group]
        for k in sectors:
            sector_row[k] = rows
            rows += up(SECTOR[k], 16)
            for a in range(4):
                s = k - WEIGHT[a]
                if 0 <= s <= 9:
                    pieces.append((s, a, at))
                    at += RUN_PAD[s]
    return pieces, sector_row


PIECES, SECTOR_ROW = layout()


def tables():
    order = -np.ones(SORTED, np.int64)
    for s in range(10):
        rows = [r for r in range(ROWS) if bin(r).count("1") == s]
        order[RUN_OFF[s] : RUN_OFF[s] + len(rows)] = rows
    sort = np.zeros((SORTED, ROWS), np.float32)
    for p in range(SORTED):
        if order[p] >= 0:
            sort[p, order[p]] = 1
    unsort = np.zeros((ROWS, SORTED_K), np.float32)
    unsort[:, :SORTED] = sort.T
    state = -2 * np.ones((2, TOTAL), np.int32)
    for s, a, at in PIECES:
        for i in range(RUN_SIZE[s]):
            r = int(order[RUN_OFF[s] + i])
            state[0, at + i] = r * 4 + a
            state[1, at + i] = (r % 128) + 128 * a + 512 * (r // 128)
    return sort, unsort, state


SORT, UNSORT, STATE = tables()


def dot(a, b):
    return jnp.dot(a, b, preferred_element_type=F32)


def lane_iota(rows):
    return lax.broadcasted_iota(jnp.int32, (rows, LANES), 1)


def halves(x):
    hi = x.astype(BF)
    return hi, (x - hi.astype(F32)).astype(BF)


def unpack_blocks(prop, blocks, bh, bl):
    for t in range(4):
        for group in (0, 7):
            blocks[t, GROUP_OFF[group] : GROUP_OFF[group] + 256, :] = jnp.zeros((256, LANES), F32)
    for k in range(GS + 1):
        n = SECTOR[k]
        if n > 100:
            period = 128 // math.gcd(n, 128)
            group = [i for i, g in enumerate(GROUPS) if g == [k]][0]
            size = GROUP_SIZE[group]
            count, stride = size // period, n * period // 128
        else:
            period, count, stride = n, 1, 1
            size = LANES
        shift_lane = SECTOR_ROW[k] - GROUP_OFF[[k in g for g in GROUPS].index(True)] if n < 100 else 0
        for i in range(period):
            start = PROP_OFF[k] + i * n
            q, r = divmod(start, 128)
            tiles = size // LANES
            lanes = lane_iota(count)
            rolled = []
            for t in range(tiles + (1 if r else 0)):
                if count > 1:
                    v = prop[pl.ds(q + t, count, stride=stride), :]
                else:
                    v = prop[q + t : q + t + 1, :]
                rolled.append(pltpu.roll(v, 128 - r, 1) if r else v)
            for t in range(tiles):
                v = jnp.where(lanes < 128 - r, rolled[t], rolled[t + 1]) if r else rolled[t]
                row = SECTOR_ROW[k] + i
                if count > 1:
                    blocks[t, pl.ds(row, count, stride=period), :] = v
                else:
                    v = jnp.where(lanes < n, v, 0.0)
                    base, within = divmod(shift_lane, 128)
                    if within:
                        v = pltpu.roll(v, within, 1)
                    blocks[base, row : row + 1, :] = v
    for group, size in enumerate(GROUP_SIZE):
        rows = slice(GROUP_OFF[group], GROUP_OFF[group] + size)
        for t in range(size // LANES):
            hi, lo = halves(blocks[t, rows, :])
            bh[rows, t * LANES : (t + 1) * LANES] = hi
            bl[rows, t * LANES : (t + 1) * LANES] = lo


def apply_gate(x, form, gate, refs):
    sort, unsort, state_lane, state_col, c_lane, c_col, bh, bl, xin, yin, sorted_out = refs
    hi, lo = halves(x)
    ordered = dot(sort[...], jnp.concatenate([hi, lo], axis=1))
    oh, ol = ordered[:, :LANES], ordered[:, LANES:]
    lanes = lane_iota(SORTED)
    for a in range(4):
        ra = pltpu.roll(oh, 128 - 32 * a, 1) if a else oh
        rb = pltpu.roll(ol, (160 - 32 * a) % 128, 1) if (160 - 32 * a) % 128 else ol
        mixed = jnp.where(lanes < 32, ra, jnp.where(lanes < 64, rb, 0.0)).astype(BF)
        for s, own, at in PIECES:
            if own == a:
                xin[at : at + RUN_PAD[s], :] = mixed[RUN_OFF[s] : RUN_OFF[s] + RUN_PAD[s], :]
    for group, size in enumerate(GROUP_SIZE):
        rows = slice(GROUP_OFF[group], GROUP_OFF[group] + size)
        spread = jnp.broadcast_to(c_col[rows, gate : gate + 1], (size, size))
        across = jnp.broadcast_to(state_lane[form : form + 1, rows], (size, size))
        pick = jnp.where(spread == across, 1.0, 0.0).astype(BF)
        z = dot(pick, xin[rows, :]).astype(BF)
        t = dot(bh[rows, :size], z) + dot(bl[rows, :size], z)
        lane = lane_iota(size)
        y = jnp.where(lane < 32, t + pltpu.roll(t, 96, 1), t + pltpu.roll(t, 32, 1))
        yh = y.astype(BF).astype(F32)
        y2 = jnp.where(lane < 32, yh, jnp.where(lane < 64, y - yh, 0.0)).astype(BF)
        spread = jnp.broadcast_to(state_col[rows, form : form + 1], (size, size))
        across = jnp.broadcast_to(c_lane[gate : gate + 1, rows], (size, size))
        place = jnp.where(spread == across, 1.0, 0.0).astype(BF)
        yin[rows, :] = dot(place, y2)
    for s in range(10):
        lanes = lane_iota(RUN_PAD[s])
        hi = lo = None
        for run, a, at in PIECES:
            if run == s:
                w = yin[at : at + RUN_PAD[s], :]
                h = pltpu.roll(w, 32 * a, 1) if a else w
                l = pltpu.roll(w, (32 * a + 96) % 128, 1) if a != 1 else w
                own = (lanes >= 32 * a) & (lanes < 32 * a + 32)
                hi = h if hi is None else jnp.where(own, h, hi)
                lo = l if lo is None else jnp.where(own, l, lo)
        sorted_out[RUN_OFF[s] : RUN_OFF[s] + RUN_PAD[s], :] = jnp.concatenate([hi, lo], axis=1).astype(BF)
    result = dot(unsort[...], sorted_out[...])
    return result[:, :LANES] + result[:, LANES:]


def to_low(x_ref):
    parts = []
    for h1 in range(4):
        stack = [x_ref[pl.ds(h1 * 4 + a, 32, stride=16), :] for a in range(4)]
        parts.append(jnp.transpose(jnp.concatenate(stack, axis=0)))
    return jnp.concatenate(parts, axis=0)


def from_low(x, x_ref):
    for h1 in range(4):
        turned = jnp.transpose(x[h1 * 128 : (h1 + 1) * 128, :])
        for a in range(4):
            x_ref[pl.ds(h1 * 4 + a, 32, stride=16), :] = turned[32 * a : 32 * a + 32, :]


def run_gates(gates, x, out, refs):
    xin, sorted_out = refs[8], refs[10]
    xin[...] = jnp.zeros(xin.shape, BF)
    sorted_out[...] = jnp.zeros(sorted_out.shape, BF)
    for gate in gates:
        if gate in (1, 3, 5):
            from_low(apply_gate(to_low(x), 1, gate, refs), out)
        else:
            out[...] = apply_gate(x[...], 0, gate, refs)
        x = out


def spin(index, position):
    return (1 - 2 * (jnp.right_shift(index, position) & 1)).astype(F32)


def phase(high_ref, level):
    high = high_ref[0]
    lane = lax.broadcasted_iota(jnp.int32, (1, LANES), 1)
    row = lax.broadcasted_iota(jnp.int32, (ROWS, 1), 0)
    lv = [level[s].astype(F32) for s in range(level.shape[0])]
    lane_z = [spin(lane, s) for s in range(7)]
    row_z = [spin(row, s) for s in range(9)]
    lane_e = sum(lv[s] * lane_z[s] * lane_z[s + 1] for s in range(6))
    row_e = sum(lv[7 + s] * row_z[s] * row_z[s + 1] for s in range(8))
    row_e = row_e + row_z[8] * (lv[LB - 1] * spin(high, 0))
    for s in range(level.shape[0] - LB):
        row_e = row_e + lv[LB + s] * spin(high, s) * spin(high, s + 1)
    energy = lane_e + row_e + (lv[6] * row_z[0]) * lane_z[6]
    return jnp.exp(-ZZ_RATE * energy)


def first_kernel(high, level, wave, prop, sort, unsort, state_lane, state_col, c_lane, c_col, out, bh, bl, blocks, *scratch):
    unpack_blocks(prop, blocks, bh, bl)
    out[...] = wave[...] * phase(high, level)
    run_gates((0, 1), out, out, (sort, unsort, state_lane, state_col, c_lane, c_col, bh, bl) + scratch)


def later_kernel(gates, x, bh, bl, sort, unsort, state_lane, state_col, c_lane, c_col, out, *scratch):
    run_gates(gates, x, out, (sort, unsort, state_lane, state_col, c_lane, c_col, bh, bl) + scratch)


SMEM = pl.BlockSpec(memory_space=pltpu.SMEM)
VMEM = pl.BlockSpec(memory_space=pltpu.VMEM)
SCRATCH = [
    pltpu.VMEM((TOTAL, LANES), BF),
    pltpu.VMEM((TOTAL, LANES), F32),
    pltpu.VMEM((SORTED_K, 2 * LANES), BF),
]
PARAMS = pltpu.CompilerParams(vmem_limit_bytes=48 * 2**20)


def later(gates, x, bh, bl, shared):
    return pl.pallas_call(
        functools.partial(later_kernel, gates),
        out_shape=jax.ShapeDtypeStruct((ROWS, LANES), F32),
        in_specs=[VMEM] * 9,
        out_specs=VMEM,
        scratch_shapes=SCRATCH,
        compiler_params=PARAMS,
        name="gates_" + "_".join(map(str, gates)),
    )(x, bh, bl, *shared)


def regroup(x):
    narrow, wide = lax.axis_size("narrow"), lax.axis_size("wide")
    grouped = x.reshape(narrow, wide, -1)
    grouped = lax.all_to_all(grouped, "narrow", split_axis=0, concat_axis=0, tiled=True)
    grouped = lax.all_to_all(grouped, "wide", split_axis=1, concat_axis=1, tiled=True)
    return grouped.reshape(ROWS, LANES)


def shards(wavefunction, propagator, gate_orders, sector_order, bond_level):
    high = lax.axis_index("wide") * lax.axis_size("narrow") + lax.axis_index("narrow")
    source = jnp.pad(propagator, (0, SOURCE_ROWS * LANES - propagator.shape[0])).reshape(SOURCE_ROWS, LANES)
    pieces, at, row = [], 0, 0
    for k in range(GS + 1):
        gap = SECTOR_ROW[k] - at
        if gap:
            pieces.append(jnp.full((gap,), -1, jnp.int32))
        pieces.append(sector_order[row : row + SECTOR[k]])
        row += SECTOR[k]
        at = SECTOR_ROW[k] + SECTOR[k]
    pieces.append(jnp.full((TOTAL - at,), -1, jnp.int32))
    padded = jnp.concatenate(pieces)
    c = jnp.zeros((GATES, TOTAL), jnp.int32)
    for t in range(GS):
        c = c + jnp.left_shift((jnp.right_shift(padded, t) & 1)[None, :], gate_orders[:, t][:, None])
    c = jnp.where(padded[None, :] < 0, -1, c)
    shared = (
        jnp.asarray(SORT, BF),
        jnp.asarray(UNSORT, BF),
        jnp.asarray(STATE),
        jnp.asarray(STATE.T),
        c,
        c.T,
    )
    x, bh, bl = pl.pallas_call(
        first_kernel,
        out_shape=(
            jax.ShapeDtypeStruct((ROWS, LANES), F32),
            jax.ShapeDtypeStruct((TOTAL, 512), BF),
            jax.ShapeDtypeStruct((TOTAL, 512), BF),
        ),
        in_specs=[SMEM, SMEM] + [VMEM] * 8,
        out_specs=(VMEM, VMEM, VMEM),
        scratch_shapes=[pltpu.VMEM((4, TOTAL, LANES), F32)] + SCRATCH,
        compiler_params=PARAMS,
        name="gates_0_1",
    )(high.reshape(1).astype(jnp.int32), bond_level, wavefunction.reshape(ROWS, LANES), source, *shared)
    x = regroup(x)
    x = later((2,), x, bh, bl, shared)
    x = regroup(x)
    x = later((3, 4, 5), x, bh, bl, shared)
    return x.reshape(-1)


def solution(mesh):
    in_specs = (P(("wide", "narrow")), P(), P(), P(), P())
    out_specs = P(("wide", "narrow"))
    return jax.shard_map(shards, mesh=mesh, in_specs=in_specs, out_specs=out_specs, check_vma=False)
```

```python
import collections
import functools
import math

import jax
import jax.numpy as jnp
import numpy as np
from jax import lax
from jax.experimental import pallas as pl
from jax.experimental.pallas import tpu as pltpu
from jax.sharding import PartitionSpec as P

LB = 16
GS = 11
GATES = 6
ZZ_RATE = 0.06
LANES = 128
ROWS = 512
BF = jnp.bfloat16
F32 = jnp.float32


def up(value, unit):
    return -(-value // unit) * unit


RUN_SIZE = [math.comb(9, s) for s in range(10)]
RUN_PAD = [up(n, 16) for n in RUN_SIZE]
RUN_OFF = [sum(RUN_PAD[:s]) for s in range(10)]
SORTED = sum(RUN_PAD)
SORTED_K = up(SORTED, LANES)
GROUPS = [[0, 1, 2], [3], [4], [5], [6], [7], [8], [9, 10, 11]]
GROUP_SIZE = [256, 256, 384, 512, 512, 384, 256, 256]
GROUP_OFF = [sum(GROUP_SIZE[:i]) for i in range(8)]
TOTAL = sum(GROUP_SIZE)
SECTOR = [math.comb(GS, k) for k in range(GS + 1)]
PROP_OFF = [sum(n * n for n in SECTOR[:k]) for k in range(GS + 1)]
SOURCE_ROWS = 5640
WEIGHT = [0, 1, 1, 2]
J_ROWS = [96, 176, 336, 464, 464, 336, 176, 96]
ORDER = [3, 4, 2, 5, 1, 6, 0, 7]
J_LANES = [128, 256, 384, 512, 512, 384, 256, 128]
A_ROWS = [160, 208, 368, 480, 480, 368, 208, 160]


def layout():
    pieces = []
    sector_row = {}
    for group, sectors in enumerate(GROUPS):
        at = GROUP_OFF[group]
        rows = GROUP_OFF[group]
        for k in sectors:
            sector_row[k] = rows
            rows += up(SECTOR[k], 16)
            for a in range(4):
                s = k - WEIGHT[a]
                if 0 <= s <= 9:
                    pieces.append((s, a, at))
                    at += RUN_PAD[s]
    return pieces, sector_row


PIECES, SECTOR_ROW = layout()


def tables():
    order = -np.ones(SORTED, np.int64)
    for s in range(10):
        rows = [r for r in range(ROWS) if bin(r).count("1") == s]
        order[RUN_OFF[s] : RUN_OFF[s] + len(rows)] = rows
    sort = np.zeros((SORTED, ROWS), np.float32)
    for p in range(SORTED):
        if order[p] >= 0:
            sort[p, order[p]] = 1
    unsort = np.zeros((ROWS, SORTED_K), np.float32)
    unsort[:, :SORTED] = sort.T
    state = -2 * np.ones((2, TOTAL), np.int32)
    for s, a, at in PIECES:
        for i in range(RUN_SIZE[s]):
            r = int(order[RUN_OFF[s] + i])
            state[0, at + i] = r * 4 + a
            state[1, at + i] = (r % 128) + 128 * a + 512 * (r // 128)
    return sort, unsort, state


SORT, UNSORT, STATE = tables()


def dot(a, b):
    return jnp.dot(a, b, preferred_element_type=F32)


def lane_iota(rows):
    return lax.broadcasted_iota(jnp.int32, (rows, LANES), 1)


def halves(x):
    hi = x.astype(BF)
    return hi, (x - hi.astype(F32)).astype(BF)


def unpack_blocks(prop, blocks, outs):
    for t in range(4):
        for group in (0, 7):
            blocks[t, GROUP_OFF[group] : GROUP_OFF[group] + 256, :] = jnp.zeros((256, LANES), F32)
    for k in range(GS + 1):
        n = SECTOR[k]
        if n > 100:
            period = 128 // math.gcd(n, 128)
            group = [i for i, g in enumerate(GROUPS) if g == [k]][0]
            size = GROUP_SIZE[group]
            count, stride = size // period, n * period // 128
        else:
            period, count, stride = n, 1, 1
            size = LANES
        shift_lane = SECTOR_ROW[k] - GROUP_OFF[[k in g for g in GROUPS].index(True)] if n < 100 else 0
        for i in range(period):
            start = PROP_OFF[k] + i * n
            q, r = divmod(start, 128)
            tiles = size // LANES
            lanes = lane_iota(count)
            rolled = []
            for t in range(tiles + (1 if r else 0)):
                if count > 1:
                    v = prop[pl.ds(q + t, count, stride=stride), :]
                else:
                    v = prop[q + t : q + t + 1, :]
                rolled.append(pltpu.roll(v, 128 - r, 1) if r else v)
            for t in range(tiles):
                v = jnp.where(lanes < 128 - r, rolled[t], rolled[t + 1]) if r else rolled[t]
                row = SECTOR_ROW[k] + i
                if count > 1:
                    blocks[t, pl.ds(row, count, stride=period), :] = v
                else:
                    v = jnp.where(lanes < n, v, 0.0)
                    base, within = divmod(shift_lane, 128)
                    if within:
                        v = pltpu.roll(v, within, 1)
                    blocks[base, row : row + 1, :] = v
    for group in range(8):
        rows = slice(GROUP_OFF[group], GROUP_OFF[group] + J_ROWS[group])
        width = J_LANES[group]
        for t in range(width // LANES):
            hi, lo = halves(blocks[t, rows, :])
            outs[group][:, t * LANES : (t + 1) * LANES] = hi
            outs[group][:, width + t * LANES : width + (t + 1) * LANES] = lo


def tile_rows(value, rows):
    return jnp.concatenate([value] * (rows // 16), axis=0)


def equal(column, across, rows, width):
    spread = jnp.broadcast_to(column, (rows, LANES)).astype(jnp.int16)
    spread = jnp.concatenate([spread] * (width // LANES), axis=1)
    return jnp.where(spread == tile_rows(across, rows), jnp.ones((), BF), jnp.zeros((), BF))


def pick_matrix(form, gate, group, refs):
    at, rows, width = GROUP_OFF[group], J_ROWS[group], GROUP_SIZE[group]
    across = refs.state16[16 * form : 16 * form + 16, at : at + width]
    return equal(refs.c_col[at : at + rows, gate : gate + 1], across, rows, width)


def place_matrix(form, gate, group, refs):
    at, rows, width = GROUP_OFF[group], A_ROWS[group], J_LANES[group]
    across = refs.c16[16 * gate : 16 * gate + 16, at : at + width]
    return equal(refs.c_col[at : at + rows, GATES + form : GATES + form + 1], across, rows, width)


def prebuild(form, gate, refs):
    for group in range(8):
        at = GROUP_OFF[group]
        refs.pick[at : at + J_ROWS[group], : GROUP_SIZE[group]] = pick_matrix(form, gate, group, refs)
        refs.place[at : at + A_ROWS[group], : J_LANES[group]] = place_matrix(form, gate, group, refs)


def fetch(refs, group):
    return pltpu.make_async_copy(refs.given[group], refs.blocks[group], refs.block_sem.at[group])


def apply_gate(x, form, gate, refs, built=False):
    xin, yin, sorted_out = refs.xin, refs.yin, refs.sorted_out
    hi, lo = halves(x)
    ordered = dot(refs.sort[...], jnp.concatenate([hi, lo], axis=1))
    oh, ol = ordered[:, :LANES], ordered[:, LANES:]
    lanes = lane_iota(SORTED)
    for a in range(4):
        ra = pltpu.roll(oh, 128 - 32 * a, 1) if a else oh
        rb = pltpu.roll(ol, (160 - 32 * a) % 128, 1) if (160 - 32 * a) % 128 else ol
        mixed = jnp.where(lanes < 32, ra, jnp.where(lanes < 64, rb, 0.0)).astype(BF)
        for s, own, at in PIECES:
            if own == a:
                xin[at : at + RUN_PAD[s], :] = mixed[RUN_OFF[s] : RUN_OFF[s] + RUN_PAD[s], :]
    zbuf, ybuf = refs.zbuf, refs.ybuf
    for group in ORDER:
        at, jr, size = GROUP_OFF[group], J_ROWS[group], GROUP_SIZE[group]
        pick = refs.pick[at : at + jr, :size] if built else pick_matrix(form, gate, group, refs)
        zbuf[at : at + jr, :] = dot(pick, xin[at : at + size, :]).astype(BF)
    for group in ORDER:
        at, jr, jl = GROUP_OFF[group], J_ROWS[group], J_LANES[group]
        if gate == 0:
            fetch(refs, group).wait()
        z = zbuf[at : at + jl, :]
        t = dot(refs.blocks[group][...], jnp.concatenate([z, z], axis=0))
        lane = lane_iota(jr)
        y = jnp.where(lane < 32, t + pltpu.roll(t, 96, 1), t + pltpu.roll(t, 32, 1))
        yh = y.astype(BF).astype(F32)
        y2 = jnp.where(lane < 32, yh, jnp.where(lane < 64, y - yh, 0.0))
        ybuf[at : at + jr, :] = y2.astype(BF)
    for group in ORDER:
        at, jl, ar = GROUP_OFF[group], J_LANES[group], A_ROWS[group]
        place = refs.place[at : at + ar, :jl] if built else place_matrix(form, gate, group, refs)
        yin[at : at + ar, :] = dot(place, ybuf[at : at + jl, :])
    for s in range(10):
        lanes = lane_iota(RUN_PAD[s])
        hi = lo = None
        for run, a, at in PIECES:
            if run == s:
                w = yin[at : at + RUN_PAD[s], :]
                h = pltpu.roll(w, 32 * a, 1) if a else w
                l = pltpu.roll(w, (32 * a + 96) % 128, 1) if a != 1 else w
                own = (lanes >= 32 * a) & (lanes < 32 * a + 32)
                hi = h if hi is None else jnp.where(own, h, hi)
                lo = l if lo is None else jnp.where(own, l, lo)
        sorted_out[RUN_OFF[s] : RUN_OFF[s] + RUN_PAD[s], :] = jnp.concatenate([hi, lo], axis=1).astype(BF)
    result = dot(refs.unsort[...], sorted_out[...])
    return result[:, :LANES] + result[:, LANES:]


def to_low(x_ref):
    parts = []
    for h1 in range(4):
        stack = [x_ref[pl.ds(h1 * 4 + a, 32, stride=16), :] for a in range(4)]
        parts.append(jnp.transpose(jnp.concatenate(stack, axis=0)))
    return jnp.concatenate(parts, axis=0)


def from_low(x, x_ref):
    for h1 in range(4):
        turned = jnp.transpose(x[h1 * 128 : (h1 + 1) * 128, :])
        for a in range(4):
            x_ref[pl.ds(h1 * 4 + a, 32, stride=16), :] = turned[32 * a : 32 * a + 32, :]


def spin(index, position):
    return (1 - 2 * (jnp.right_shift(index, position) & 1)).astype(F32)


def phase(high, level):
    lane = lax.broadcasted_iota(jnp.int32, (1, LANES), 1)
    row = lax.broadcasted_iota(jnp.int32, (ROWS, 1), 0)
    lv = [level[s].astype(F32) for s in range(level.shape[0])]
    lane_z = [spin(lane, s) for s in range(7)]
    row_z = [spin(row, s) for s in range(9)]
    lane_e = sum(lv[s] * lane_z[s] * lane_z[s + 1] for s in range(6))
    row_e = sum(lv[7 + s] * row_z[s] * row_z[s + 1] for s in range(8))
    row_e = row_e + row_z[8] * (lv[LB - 1] * spin(high, 0))
    for s in range(level.shape[0] - LB):
        row_e = row_e + lv[LB + s] * spin(high, s) * spin(high, s + 1)
    energy = lane_e + row_e + (lv[6] * row_z[0]) * lane_z[6]
    return jnp.exp(-ZZ_RATE * energy)


def padded_states(sectors):
    lane = lane_iota(1)
    tiles = []
    for tile in range(TOTAL // LANES):
        value = jnp.full((1, LANES), -1, jnp.int32)
        first = 0
        for k in range(GS + 1):
            n, begin = SECTOR[k], SECTOR_ROW[k] - tile * LANES
            low, high = max(begin, 0), min(begin + n, LANES)
            if low < high:
                q, r = divmod(first - begin, LANES)
                for step in (0, 1):
                    a, b = (low, min(high, LANES - r)) if step == 0 else (max(low, LANES - r), high)
                    if a < b:
                        row = sectors[q + step : q + step + 1, :]
                        row = pltpu.roll(row, LANES - r, 1) if r else row
                        value = jnp.where((lane >= a) & (lane < b), row, value)
            first += n
        tiles.append(value)
    return jnp.concatenate(tiles, axis=1)


def index_maps(orders, sectors, state, refs):
    states = padded_states(sectors)
    maps = []
    for g in range(GATES):
        c = jnp.zeros(states.shape, jnp.int32)
        for t in range(GS):
            c = c + jnp.left_shift(jnp.right_shift(states, t) & 1, orders[g, t])
        c = jnp.where(states < 0, -1, c)
        refs.c16[16 * g : 16 * g + 16, :] = jnp.broadcast_to(c, (16, TOTAL)).astype(jnp.int16)
        maps.append(c)
    for form in range(2):
        own = state[form : form + 1, :]
        refs.state16[16 * form : 16 * form + 16, :] = jnp.broadcast_to(own, (16, TOTAL)).astype(jnp.int16)
        maps.append(own)
    refs.c_col[...] = jnp.transpose(jnp.concatenate(maps, axis=0))


class Exchange:
    def __init__(self, wide, narrow, source, target, send_sem, recv_sem):
        self.wide, self.count = wide, wide * narrow
        self.me = lax.axis_index("narrow") * wide + lax.axis_index("wide")
        self.source, self.target, self.sems = source, target, (send_sem, recv_sem)

    def device(self, t):
        return {"wide": lax.rem(t, self.wide), "narrow": t // self.wide}

    def greet(self):
        barrier = pltpu.get_barrier_semaphore()

        @pl.loop(1, self.count)
        def _(off):
            t = lax.rem(self.me + off, self.count)
            pl.semaphore_signal(barrier, inc=1, device_id=self.device(t), device_id_type=MESH)

    def greeted(self):
        pl.semaphore_wait(pltpu.get_barrier_semaphore(), self.count - 1)

    def start(self):
        @pl.loop(1, self.count)
        def _(off):
            t = lax.rem(self.me + off, self.count)
            pltpu.make_async_remote_copy(
                src_ref=self.source.at[t],
                dst_ref=self.target.at[self.me],
                send_sem=self.sems[0],
                recv_sem=self.sems[1],
                device_id=self.device(t),
                device_id_type=MESH,
            ).start()

        self.target[pl.ds(self.me, 1)] = self.source[pl.ds(self.me, 1)]

    def wait(self):
        rest = pl.ds(0, self.count - 1)
        both = pltpu.make_async_remote_copy(
            src_ref=self.source.at[rest],
            dst_ref=self.target.at[rest],
            send_sem=self.sems[0],
            recv_sem=self.sems[1],
            device_id=self.device(lax.rem(self.me + 1, self.count)),
            device_id_type=MESH,
        )
        both.wait_send()
        both.wait_recv()


def unpack_kernel(prop, *rest):
    unpack_blocks(prop, rest[8], rest[:8])


Refs = collections.namedtuple(
    "Refs",
    ["sort", "unsort", "given", "blocks", "block_sem", "state16", "c16", "c_col"]
    + ["xin", "zbuf", "ybuf", "yin", "sorted_out", "pick", "place"],
)


def gates_kernel(wide, narrow, level, orders, wave, sectors, state, sort, unsort, *rest):
    given, out, blocks = rest[:8], rest[8], rest[9:17]
    state16, c16, c_col, xin, zbuf, ybuf, yin, sorted_out, pick, place, x, sent, landed = rest[17:30]
    block_sem, send_sem, recv_sem = rest[30:]
    refs = Refs(
        sort, unsort, given, blocks, block_sem, state16, c16, c_col,
        xin, zbuf, ybuf, yin, sorted_out, pick, place,
    )
    for group in ORDER:
        fetch(refs, group).start()
    there = Exchange(wide, narrow, sent.at[0], landed.at[0], send_sem.at[0], recv_sem.at[0])
    back = Exchange(wide, narrow, sent.at[1], landed.at[1], send_sem.at[1], recv_sem.at[1])
    shape = sent.shape[1:]
    there.greet()
    for zeroed in (xin, zbuf, ybuf):
        zeroed[...] = jnp.zeros(zeroed.shape, BF)
    sorted_out[...] = jnp.zeros(sorted_out.shape, BF)
    index_maps(orders, sectors, state, refs)
    high = lax.axis_index("wide") * narrow + lax.axis_index("narrow")
    x[...] = apply_gate(wave[...] * phase(high, level), 0, 0, refs)
    from_low(apply_gate(to_low(x), 1, 1, refs), x)
    sent[0] = x[...].reshape(shape)
    there.greeted()
    there.start()
    prebuild(0, 2, refs)
    there.wait()
    sent[1] = apply_gate(landed[0].reshape(ROWS, LANES), 0, 2, refs, True).reshape(shape)
    back.start()
    prebuild(1, 3, refs)
    back.wait()
    x[...] = landed[1].reshape(ROWS, LANES)
    from_low(apply_gate(to_low(x), 1, 3, refs, True), x)
    x[...] = apply_gate(x[...], 0, 4, refs)
    from_low(apply_gate(to_low(x), 1, 5, refs), out)


SMEM = pl.BlockSpec(memory_space=pltpu.SMEM)
VMEM = pl.BlockSpec(memory_space=pltpu.VMEM)
MESH = pl.DeviceIdType.MESH


def shards(wavefunction, propagator, gate_orders, sector_order, bond_level):
    wide, narrow = lax.axis_size("wide"), lax.axis_size("narrow")
    count = wide * narrow
    source = jnp.pad(propagator, (0, SOURCE_ROWS * LANES - propagator.shape[0])).reshape(SOURCE_ROWS, LANES)
    shapes = [(J_ROWS[g], 2 * J_LANES[g]) for g in range(8)]
    blocks = pl.pallas_call(
        unpack_kernel,
        out_shape=[jax.ShapeDtypeStruct(shape, BF) for shape in shapes],
        in_specs=[VMEM],
        out_specs=[VMEM] * 8,
        scratch_shapes=[pltpu.VMEM((4, TOTAL, LANES), F32)],
        compiler_params=pltpu.CompilerParams(vmem_limit_bytes=32 * 2**20),
        name="unpack_blocks",
    )(source)
    x = pl.pallas_call(
        functools.partial(gates_kernel, wide, narrow),
        out_shape=jax.ShapeDtypeStruct((ROWS, LANES), F32),
        in_specs=[SMEM, SMEM] + [VMEM] * 5 + [pl.BlockSpec(memory_space=pl.ANY)] * 8,
        out_specs=VMEM,
        scratch_shapes=[pltpu.VMEM(shape, BF) for shape in shapes]
        + [
            pltpu.VMEM((32, TOTAL), jnp.int16),
            pltpu.VMEM((16 * GATES, TOTAL), jnp.int16),
            pltpu.VMEM((TOTAL, 8), jnp.int32),
            pltpu.VMEM((TOTAL, LANES), BF),
            pltpu.VMEM((TOTAL, LANES), BF),
            pltpu.VMEM((TOTAL, LANES), BF),
            pltpu.VMEM((TOTAL, LANES), F32),
            pltpu.VMEM((SORTED_K, 2 * LANES), BF),
            pltpu.VMEM((TOTAL, 512), BF),
            pltpu.VMEM((TOTAL, 512), BF),
            pltpu.VMEM((ROWS, LANES), F32),
            pltpu.VMEM((2, count, ROWS // count, LANES), F32),
            pltpu.VMEM((2, count, ROWS // count, LANES), F32),
            pltpu.SemaphoreType.DMA((8,)),
            pltpu.SemaphoreType.DMA((2,)),
            pltpu.SemaphoreType.DMA((2,)),
        ],
        compiler_params=pltpu.CompilerParams(
            vmem_limit_bytes=44 * 2**20, collective_id=0, has_side_effects=True
        ),
        name="six_gates",
    )(
        bond_level,
        gate_orders,
        wavefunction.reshape(ROWS, LANES),
        sector_order.reshape(-1, LANES),
        jnp.asarray(STATE),
        jnp.asarray(SORT, BF),
        jnp.asarray(UNSORT, BF),
        *blocks,
    )
    return x.reshape(-1)


def solution(mesh):
    in_specs = (P(("wide", "narrow")), P(), P(), P(), P())
    out_specs = P(("wide", "narrow"))
    return jax.shard_map(shards, mesh=mesh, in_specs=in_specs, out_specs=out_specs, check_vma=False)
```

```python
import collections
import functools
import math

import jax
import jax.numpy as jnp
import numpy as np
from jax import lax
from jax.experimental import pallas as pl
from jax.experimental.pallas import tpu as pltpu
from jax.sharding import PartitionSpec as P

LB = 16
GS = 11
GATES = 6
ZZ_RATE = 0.06
LANES = 128
ROWS = 512
BF = jnp.bfloat16
F32 = jnp.float32


def up(value, unit):
    return -(-value // unit) * unit


RUN_SIZE = [math.comb(9, s) for s in range(10)]
RUN_PAD = [up(n, 16) for n in RUN_SIZE]
RUN_OFF = [sum(RUN_PAD[:s]) for s in range(10)]
SORTED = sum(RUN_PAD)
SORTED_K = up(SORTED, LANES)
GROUPS = [[0, 1, 2], [3], [4], [5], [6], [7], [8], [9, 10, 11]]
GROUP_SIZE = [256, 256, 384, 512, 512, 384, 256, 256]
GROUP_OFF = [sum(GROUP_SIZE[:i]) for i in range(8)]
TOTAL = sum(GROUP_SIZE)
SECTOR = [math.comb(GS, k) for k in range(GS + 1)]
PROP_OFF = [sum(n * n for n in SECTOR[:k]) for k in range(GS + 1)]
SOURCE_ROWS = 5640
WEIGHT = [0, 1, 1, 2]
J_ROWS = [96, 176, 336, 464, 464, 336, 176, 96]
ORDER = [3, 4, 2, 5, 1, 6, 0, 7]
J_LANES = [128, 256, 384, 512, 512, 384, 256, 128]
A_ROWS = [160, 208, 368, 480, 480, 368, 208, 160]


def layout():
    pieces = []
    sector_row = {}
    for group, sectors in enumerate(GROUPS):
        at = GROUP_OFF[group]
        rows = GROUP_OFF[group]
        for k in sectors:
            sector_row[k] = rows
            rows += up(SECTOR[k], 16)
            for a in range(4):
                s = k - WEIGHT[a]
                if 0 <= s <= 9:
                    pieces.append((s, a, at))
                    at += RUN_PAD[s]
    return pieces, sector_row


PIECES, SECTOR_ROW = layout()


def tables():
    order = -np.ones(SORTED, np.int64)
    for s in range(10):
        rows = [r for r in range(ROWS) if bin(r).count("1") == s]
        order[RUN_OFF[s] : RUN_OFF[s] + len(rows)] = rows
    sort = np.zeros((SORTED, ROWS), np.float32)
    for p in range(SORTED):
        if order[p] >= 0:
            sort[p, order[p]] = 1
    unsort = np.zeros((ROWS, SORTED_K), np.float32)
    unsort[:, :SORTED] = sort.T
    state = -2 * np.ones((2, TOTAL), np.int32)
    for s, a, at in PIECES:
        for i in range(RUN_SIZE[s]):
            r = int(order[RUN_OFF[s] + i])
            state[0, at + i] = r * 4 + a
            state[1, at + i] = (r % 128) + 128 * a + 512 * (r // 128)
    return sort, unsort, state


SORT, UNSORT, STATE = tables()


def dot(a, b):
    return jnp.dot(a, b, preferred_element_type=F32)


def lane_iota(rows):
    return lax.broadcasted_iota(jnp.int32, (rows, LANES), 1)


def halves(x):
    hi = x.astype(BF)
    return hi, (x - hi.astype(F32)).astype(BF)


def unpack_blocks(prop, blocks, outs):
    for t in range(4):
        for group in (0, 7):
            blocks[t, GROUP_OFF[group] : GROUP_OFF[group] + 256, :] = jnp.zeros((256, LANES), F32)
    for k in range(GS + 1):
        n = SECTOR[k]
        if n > 100:
            period = 128 // math.gcd(n, 128)
            group = [i for i, g in enumerate(GROUPS) if g == [k]][0]
            size = GROUP_SIZE[group]
            count, stride = size // period, n * period // 128
        else:
            period, count, stride = n, 1, 1
            size = LANES
        shift_lane = SECTOR_ROW[k] - GROUP_OFF[[k in g for g in GROUPS].index(True)] if n < 100 else 0
        for i in range(period):
            start = PROP_OFF[k] + i * n
            q, r = divmod(start, 128)
            tiles = size // LANES
            lanes = lane_iota(count)
            rolled = []
            for t in range(tiles + (1 if r else 0)):
                if count > 1:
                    v = prop[pl.ds(q + t, count, stride=stride), :]
                else:
                    v = prop[q + t : q + t + 1, :]
                rolled.append(pltpu.roll(v, 128 - r, 1) if r else v)
            for t in range(tiles):
                v = jnp.where(lanes < 128 - r, rolled[t], rolled[t + 1]) if r else rolled[t]
                row = SECTOR_ROW[k] + i
                if count > 1:
                    blocks[t, pl.ds(row, count, stride=period), :] = v
                else:
                    v = jnp.where(lanes < n, v, 0.0)
                    base, within = divmod(shift_lane, 128)
                    if within:
                        v = pltpu.roll(v, within, 1)
                    blocks[base, row : row + 1, :] = v
    for group in range(8):
        rows = slice(GROUP_OFF[group], GROUP_OFF[group] + J_ROWS[group])
        width = J_LANES[group]
        for t in range(width // LANES):
            hi, lo = halves(blocks[t, rows, :])
            outs[group][:, t * LANES : (t + 1) * LANES] = hi
            outs[group][:, width + t * LANES : width + (t + 1) * LANES] = lo


def tile_rows(value, rows):
    return jnp.concatenate([value] * (rows // 16), axis=0)


def equal(column, across, rows, width):
    spread = jnp.broadcast_to(column, (rows, LANES)).astype(jnp.int16)
    spread = jnp.concatenate([spread] * (width // LANES), axis=1)
    return jnp.where(spread == tile_rows(across, rows), jnp.ones((), BF), jnp.zeros((), BF))


def pick_matrix(form, gate, group, refs):
    at, rows, width = GROUP_OFF[group], J_ROWS[group], GROUP_SIZE[group]
    across = refs.state16[16 * form : 16 * form + 16, at : at + width]
    return equal(refs.c_col[at : at + rows, gate : gate + 1], across, rows, width)


def place_matrix(form, gate, group, refs):
    at, rows, width = GROUP_OFF[group], A_ROWS[group], J_LANES[group]
    across = refs.c16[16 * gate : 16 * gate + 16, at : at + width]
    return equal(refs.c_col[at : at + rows, GATES + form : GATES + form + 1], across, rows, width)


def prebuild(form, gate, refs):
    for group in range(8):
        at = GROUP_OFF[group]
        refs.pick[gate - 2, at : at + J_ROWS[group], : GROUP_SIZE[group]] = pick_matrix(form, gate, group, refs)
        refs.place[gate - 2, at : at + A_ROWS[group], : J_LANES[group]] = place_matrix(form, gate, group, refs)


def fetch(refs, group):
    return pltpu.make_async_copy(refs.given[group], refs.blocks[group], refs.block_sem.at[group])


def apply_gate(x, form, gate, refs, built=False):
    xin, yin, sorted_out = refs.xin, refs.yin, refs.sorted_out
    hi, lo = halves(x)
    ordered = dot(refs.sort[...], jnp.concatenate([hi, lo], axis=1))
    oh, ol = ordered[:, :LANES], ordered[:, LANES:]
    lanes = lane_iota(SORTED)
    for a in range(4):
        ra = pltpu.roll(oh, 128 - 32 * a, 1) if a else oh
        rb = pltpu.roll(ol, (160 - 32 * a) % 128, 1) if (160 - 32 * a) % 128 else ol
        mixed = jnp.where(lanes < 32, ra, jnp.where(lanes < 64, rb, 0.0)).astype(BF)
        for s, own, at in PIECES:
            if own == a:
                xin[at : at + RUN_PAD[s], :] = mixed[RUN_OFF[s] : RUN_OFF[s] + RUN_PAD[s], :]
    zbuf, ybuf = refs.zbuf, refs.ybuf
    for group in ORDER:
        at, jr, size = GROUP_OFF[group], J_ROWS[group], GROUP_SIZE[group]
        pick = refs.pick[gate - 2, at : at + jr, :size] if built else pick_matrix(form, gate, group, refs)
        zbuf[at : at + jr, :] = dot(pick, xin[at : at + size, :]).astype(BF)
    for group in ORDER:
        at, jr, jl = GROUP_OFF[group], J_ROWS[group], J_LANES[group]
        if gate == 0:
            fetch(refs, group).wait()
        z = zbuf[at : at + jl, :]
        t = dot(refs.blocks[group][...], jnp.concatenate([z, z], axis=0))
        lane = lane_iota(jr)
        y = jnp.where(lane < 32, t + pltpu.roll(t, 96, 1), t + pltpu.roll(t, 32, 1))
        yh = y.astype(BF).astype(F32)
        y2 = jnp.where(lane < 32, yh, jnp.where(lane < 64, y - yh, 0.0))
        ybuf[at : at + jr, :] = y2.astype(BF)
    for group in ORDER:
        at, jl, ar = GROUP_OFF[group], J_LANES[group], A_ROWS[group]
        place = refs.place[gate - 2, at : at + ar, :jl] if built else place_matrix(form, gate, group, refs)
        yin[at : at + ar, :] = dot(place, ybuf[at : at + jl, :])
    for s in range(10):
        lanes = lane_iota(RUN_PAD[s])
        hi = lo = None
        for run, a, at in PIECES:
            if run == s:
                w = yin[at : at + RUN_PAD[s], :]
                h = pltpu.roll(w, 32 * a, 1) if a else w
                l = pltpu.roll(w, (32 * a + 96) % 128, 1) if a != 1 else w
                own = (lanes >= 32 * a) & (lanes < 32 * a + 32)
                hi = h if hi is None else jnp.where(own, h, hi)
                lo = l if lo is None else jnp.where(own, l, lo)
        sorted_out[RUN_OFF[s] : RUN_OFF[s] + RUN_PAD[s], :] = jnp.concatenate([hi, lo], axis=1).astype(BF)
    result = dot(refs.unsort[...], sorted_out[...])
    return result[:, :LANES] + result[:, LANES:]


def to_low(x_ref):
    parts = []
    for h1 in range(4):
        stack = [x_ref[pl.ds(h1 * 4 + a, 32, stride=16), :] for a in range(4)]
        parts.append(jnp.transpose(jnp.concatenate(stack, axis=0)))
    return jnp.concatenate(parts, axis=0)


def from_low(x, x_ref):
    for h1 in range(4):
        turned = jnp.transpose(x[h1 * 128 : (h1 + 1) * 128, :])
        for a in range(4):
            x_ref[pl.ds(h1 * 4 + a, 32, stride=16), :] = turned[32 * a : 32 * a + 32, :]


def spin(index, position):
    return (1 - 2 * (jnp.right_shift(index, position) & 1)).astype(F32)


def phase(high, level):
    lane = lax.broadcasted_iota(jnp.int32, (1, LANES), 1)
    row = lax.broadcasted_iota(jnp.int32, (ROWS, 1), 0)
    lv = [level[s].astype(F32) for s in range(level.shape[0])]
    lane_z = [spin(lane, s) for s in range(7)]
    row_z = [spin(row, s) for s in range(9)]
    lane_e = sum(lv[s] * lane_z[s] * lane_z[s + 1] for s in range(6))
    row_e = sum(lv[7 + s] * row_z[s] * row_z[s + 1] for s in range(8))
    row_e = row_e + row_z[8] * (lv[LB - 1] * spin(high, 0))
    for s in range(level.shape[0] - LB):
        row_e = row_e + lv[LB + s] * spin(high, s) * spin(high, s + 1)
    energy = lane_e + row_e + (lv[6] * row_z[0]) * lane_z[6]
    return jnp.exp(-ZZ_RATE * energy)


def padded_states(sectors):
    lane = lane_iota(1)
    tiles = []
    for tile in range(TOTAL // LANES):
        value = jnp.full((1, LANES), -1, jnp.int32)
        first = 0
        for k in range(GS + 1):
            n, begin = SECTOR[k], SECTOR_ROW[k] - tile * LANES
            low, high = max(begin, 0), min(begin + n, LANES)
            if low < high:
                q, r = divmod(first - begin, LANES)
                for step in (0, 1):
                    a, b = (low, min(high, LANES - r)) if step == 0 else (max(low, LANES - r), high)
                    if a < b:
                        row = sectors[q + step : q + step + 1, :]
                        row = pltpu.roll(row, LANES - r, 1) if r else row
                        value = jnp.where((lane >= a) & (lane < b), row, value)
            first += n
        tiles.append(value)
    return jnp.concatenate(tiles, axis=1)


def index_maps(orders, sectors, state, refs):
    states = padded_states(sectors)
    maps = []
    for g in range(GATES):
        c = jnp.zeros(states.shape, jnp.int32)
        for t in range(GS):
            c = c + jnp.left_shift(jnp.right_shift(states, t) & 1, orders[g, t])
        c = jnp.where(states < 0, -1, c)
        refs.c16[16 * g : 16 * g + 16, :] = jnp.broadcast_to(c, (16, TOTAL)).astype(jnp.int16)
        maps.append(c)
    for form in range(2):
        own = state[form : form + 1, :]
        refs.state16[16 * form : 16 * form + 16, :] = jnp.broadcast_to(own, (16, TOTAL)).astype(jnp.int16)
        maps.append(own)
    refs.c_col[...] = jnp.transpose(jnp.concatenate(maps, axis=0))


class Exchange:
    def __init__(self, wide, narrow, source, target, send_sem, recv_sem):
        self.wide, self.count = wide, wide * narrow
        self.me = lax.axis_index("narrow") * wide + lax.axis_index("wide")
        self.source, self.target, self.sems = source, target, (send_sem, recv_sem)

    def device(self, t):
        return {"wide": lax.rem(t, self.wide), "narrow": t // self.wide}

    def greet(self):
        barrier = pltpu.get_barrier_semaphore()

        @pl.loop(1, self.count)
        def _(off):
            t = lax.rem(self.me + off, self.count)
            pl.semaphore_signal(barrier, inc=1, device_id=self.device(t), device_id_type=MESH)

    def greeted(self):
        pl.semaphore_wait(pltpu.get_barrier_semaphore(), self.count - 1)

    def start(self):
        @pl.loop(1, self.count)
        def _(off):
            t = lax.rem(self.me + off, self.count)
            pltpu.make_async_remote_copy(
                src_ref=self.source.at[t],
                dst_ref=self.target.at[self.me],
                send_sem=self.sems[0],
                recv_sem=self.sems[1],
                device_id=self.device(t),
                device_id_type=MESH,
            ).start()

        self.target[pl.ds(self.me, 1)] = self.source[pl.ds(self.me, 1)]

    def wait(self):
        rest = pl.ds(0, self.count - 1)
        both = pltpu.make_async_remote_copy(
            src_ref=self.source.at[rest],
            dst_ref=self.target.at[rest],
            send_sem=self.sems[0],
            recv_sem=self.sems[1],
            device_id=self.device(lax.rem(self.me + 1, self.count)),
            device_id_type=MESH,
        )
        both.wait_send()
        both.wait_recv()


def unpack_kernel(prop, *rest):
    unpack_blocks(prop, rest[8], rest[:8])


Refs = collections.namedtuple(
    "Refs",
    ["sort", "unsort", "given", "blocks", "block_sem", "state16", "c16", "c_col"]
    + ["xin", "zbuf", "ybuf", "yin", "sorted_out", "pick", "place"],
)


def gates_kernel(wide, narrow, level, orders, wave, sectors, state, sort, unsort, *rest):
    given, out, blocks = rest[:8], rest[8], rest[9:17]
    state16, c16, c_col, xin, zbuf, ybuf, yin, sorted_out, pick, place, x, sent, landed = rest[17:30]
    block_sem, send_sem, recv_sem = rest[30:]
    refs = Refs(
        sort, unsort, given, blocks, block_sem, state16, c16, c_col,
        xin, zbuf, ybuf, yin, sorted_out, pick, place,
    )
    for group in ORDER:
        fetch(refs, group).start()
    there = Exchange(wide, narrow, sent.at[0], landed.at[0], send_sem.at[0], recv_sem.at[0])
    back = Exchange(wide, narrow, sent.at[1], landed.at[1], send_sem.at[1], recv_sem.at[1])
    shape = sent.shape[1:]
    there.greet()
    for zeroed in (xin, zbuf, ybuf):
        zeroed[...] = jnp.zeros(zeroed.shape, BF)
    sorted_out[...] = jnp.zeros(sorted_out.shape, BF)
    index_maps(orders, sectors, state, refs)
    high = lax.axis_index("wide") * narrow + lax.axis_index("narrow")
    x[...] = apply_gate(wave[...] * phase(high, level), 0, 0, refs)
    from_low(apply_gate(to_low(x), 1, 1, refs), x)
    sent[0] = x[...].reshape(shape)
    there.greeted()
    there.start()
    prebuild(0, 2, refs)
    prebuild(0, 4, refs)
    there.wait()
    sent[1] = apply_gate(landed[0].reshape(ROWS, LANES), 0, 2, refs, True).reshape(shape)
    back.start()
    prebuild(1, 3, refs)
    prebuild(1, 5, refs)
    back.wait()
    x[...] = landed[1].reshape(ROWS, LANES)
    from_low(apply_gate(to_low(x), 1, 3, refs, True), x)
    x[...] = apply_gate(x[...], 0, 4, refs, True)
    from_low(apply_gate(to_low(x), 1, 5, refs, True), out)


SMEM = pl.BlockSpec(memory_space=pltpu.SMEM)
VMEM = pl.BlockSpec(memory_space=pltpu.VMEM)
MESH = pl.DeviceIdType.MESH


def shards(wavefunction, propagator, gate_orders, sector_order, bond_level):
    wide, narrow = lax.axis_size("wide"), lax.axis_size("narrow")
    count = wide * narrow
    source = jnp.pad(propagator, (0, SOURCE_ROWS * LANES - propagator.shape[0])).reshape(SOURCE_ROWS, LANES)
    shapes = [(J_ROWS[g], 2 * J_LANES[g]) for g in range(8)]
    blocks = pl.pallas_call(
        unpack_kernel,
        out_shape=[jax.ShapeDtypeStruct(shape, BF) for shape in shapes],
        in_specs=[VMEM],
        out_specs=[VMEM] * 8,
        scratch_shapes=[pltpu.VMEM((4, TOTAL, LANES), F32)],
        compiler_params=pltpu.CompilerParams(vmem_limit_bytes=32 * 2**20),
        name="unpack_blocks",
    )(source)
    x = pl.pallas_call(
        functools.partial(gates_kernel, wide, narrow),
        out_shape=jax.ShapeDtypeStruct((ROWS, LANES), F32),
        in_specs=[SMEM, SMEM] + [VMEM] * 5 + [pl.BlockSpec(memory_space=pl.ANY)] * 8,
        out_specs=VMEM,
        scratch_shapes=[pltpu.VMEM(shape, BF) for shape in shapes]
        + [
            pltpu.VMEM((32, TOTAL), jnp.int16),
            pltpu.VMEM((16 * GATES, TOTAL), jnp.int16),
            pltpu.VMEM((TOTAL, 8), jnp.int32),
            pltpu.VMEM((TOTAL, LANES), BF),
            pltpu.VMEM((TOTAL, LANES), BF),
            pltpu.VMEM((TOTAL, LANES), BF),
            pltpu.VMEM((TOTAL, LANES), F32),
            pltpu.VMEM((SORTED_K, 2 * LANES), BF),
            pltpu.VMEM((GATES - 2, TOTAL, 512), BF),
            pltpu.VMEM((GATES - 2, TOTAL, 512), BF),
            pltpu.VMEM((ROWS, LANES), F32),
            pltpu.VMEM((2, count, ROWS // count, LANES), F32),
            pltpu.VMEM((2, count, ROWS // count, LANES), F32),
            pltpu.SemaphoreType.DMA((8,)),
            pltpu.SemaphoreType.DMA((2,)),
            pltpu.SemaphoreType.DMA((2,)),
        ],
        compiler_params=pltpu.CompilerParams(
            vmem_limit_bytes=44 * 2**20, collective_id=0, has_side_effects=True
        ),
        name="six_gates",
    )(
        bond_level,
        gate_orders,
        wavefunction.reshape(ROWS, LANES),
        sector_order.reshape(-1, LANES),
        jnp.asarray(STATE),
        jnp.asarray(SORT, BF),
        jnp.asarray(UNSORT, BF),
        *blocks,
    )
    return x.reshape(-1)


def solution(mesh):
    in_specs = (P(("wide", "narrow")), P(), P(), P(), P())
    out_specs = P(("wide", "narrow"))
    return jax.shard_map(shards, mesh=mesh, in_specs=in_specs, out_specs=out_specs, check_vma=False)
```
